512 devices in a mesh: ctx: 16 (over z_hi, y), head: 8 (over x, core), req: 4 (over z_lo).
Axes of the slice: x: 4, y: 8, z: 8 (z_hi: 2, z_lo: 4; z = z_hi * 4 + z_lo), core: 2. Of those that a mesh axis runs over, the one named last changes fastest.
Arguments:
- queries: bfloat16 [16384, 8192], P(('req', 'ctx'), 'head'), parts along dimension 0, may hold values from -5 to 5
- keys: bfloat16 [16384, 1024], P(('req', 'ctx'), 'head'), parts along dimension 0, may hold values from -5 to 5
- values: bfloat16 [16384, 1024], P(('req', 'ctx'), 'head'), parts along dimension 0, may hold values from -6 to 6
- block_order: int32 [128], P('req'), parts along dimension 0, may hold values from 0 to 31, each once
- owner_of: int32 [64], P('req'), parts along dimension 0, may hold values from 0 to 3, as said below
- dec_queries: bfloat16 [16, 128, 8192], P('req', None, 'head'), parts along dimension 0, may hold values from -5 to 5
- dec_pos: int32 [16, 128], P('req'), parts along dimension 0, may hold values from 1 to 4096, as said below
Outputs:
- attn_out: bfloat16 [16384, 8192], P(('req', 'ctx'), 'head'), parts along dimension 0
- owned_keys: bfloat16 [16384, 1024], P(('req', 'ctx'), 'head'), parts along dimension 0
- owned_values: bfloat16 [16384, 1024], P(('req', 'ctx'), 'head'), parts along dimension 0
- dec_out: bfloat16 [16, 128, 8192], P('req', 'ctx', 'head'), parts along dimension 0
The draws below stay inside these ranges and needn't reach their ends.
There are 4 independent parts, one for each index of `req`. The reference program is written for one: setup_inputs(seed, part) draws one part's arguments, and reference() takes and returns one part's arrays. A program takes and returns all parts, laid end to end along the dimension named above; each array names one. Nothing has to cross between parts.
Inputs may be any that keep to these rules, and one draw needn't show every extreme that they name: `owner_of`: each owner group is named by exactly 4 ranks. `dec_pos`: every step has rows that read all 4096 positions and a row that reads one position.
All inputs are finite; a program needn't handle non-finite values.
Results may differ from the reference program's by a relative error of at most 0.023.
Values may be sent and summed in bfloat16 or wider, within the bound.
No kernel may reach another device: no remote copies, remote signals or barrier semaphores. Data moves between devices by JAX's collectives and lax.ppermute only.
A program may use at most 64 MiB of HBM per device.

```python
import math
import jax
import jax.numpy as jnp
from jax import lax

HQ = 64
KVH = 8
HD = 128
TOK_DEV = 256
DROWS = 128
STEPS = 4
OWNERS = 4
RANKS = 16
BLOCKS = 32
BLK = 128
SEQ = 4096


def draw_keys(key, part):
    key = jax.random.fold_in(key, 1)
    field = jnp.clip(jax.random.normal(key, (SEQ, KVH * HD), jnp.float32), -5.0, 5.0)
    return field.astype(jnp.bfloat16)


def draw_queries(key, part):
    key = jax.random.fold_in(key, 2)
    field = jnp.clip(jax.random.normal(key, (SEQ, HQ * HD), jnp.float32), -5.0, 5.0)
    return field.astype(jnp.bfloat16)


def draw_dec_queries(key, part):
    key = jax.random.fold_in(key, 3)
    field = jnp.clip(jax.random.normal(key, (STEPS, DROWS, HQ * HD), jnp.float32), -5.0, 5.0)
    return field.astype(jnp.bfloat16)


def draw_dec_pos(key, part):
    key = jax.random.fold_in(key, 4)
    limits = jax.random.randint(key, (STEPS, DROWS), 1, SEQ + 1, jnp.int32)
    limits = limits.at[:, 0:4].set(SEQ).at[:, 4].set(1)
    return limits.astype(jnp.int32)


def order_within(scores, member):
    lower = (scores[None, :] < scores[:, None]) & member[None, :]
    return jnp.sum(lower.astype(jnp.int32), axis=1)


def draw_owner_of(key, part):
    key = jax.random.fold_in(key, 5)
    pick_key, score_key, rest_key = jax.random.split(key, 3)
    size_group = RANKS // OWNERS
    ranks = jnp.arange(RANKS, dtype=jnp.int32)
    first = jax.random.randint(pick_key, (), 0, RANKS, jnp.int32)
    target = (first + RANKS // 2) % RANKS
    chosen_group = target // size_group
    need_below = target % size_group
    need_above = size_group - 1 - need_below
    scores = jax.random.randint(score_key, (RANKS,), 0, 1 << 20, jnp.int32) * RANKS + ranks
    below = ranks < first
    above = ranks > first
    place_below = order_within(scores, below)
    place_above = order_within(scores, above)
    chosen = (ranks == first) | below & (place_below < need_below) | above & (place_above < need_above)
    rest = jnp.logical_not(chosen)
    rest_scores = jax.random.randint(rest_key, (RANKS,), 0, 1 << 20, jnp.int32) * RANKS + ranks
    place_rest = order_within(rest_scores, rest)
    label = place_rest // size_group
    label = label + (label >= chosen_group).astype(jnp.int32)
    return jnp.where(chosen, chosen_group, label).astype(jnp.int32)


def level_of(key, dims, pieces, smallest, largest):
    factor_of = 1.0
    for position, parts in pieces:
        steps = jax.random.uniform(jax.random.fold_in(jax.random.fold_in(key, 6), position), (parts,), jnp.float32, smallest / len(pieces), largest / len(pieces))
        factor_of = factor_of * jnp.repeat(jnp.exp(steps), dims[position] // parts).reshape((-1,) + (1,) * (len(dims) - 1 - position))
    return factor_of


def noise(key, extent, spread, bound, shards=(), kind=jnp.bfloat16):
    values = jax.random.normal(key, extent, jnp.float32) * spread
    if len(shards) > 0:
        values = level_of(key, extent, shards, -0.22, 0.18) * values
    return jnp.clip(values, min=-bound, max=bound).astype(kind)


def setup_inputs(seed: int = 0, part: int = 0) -> dict:
    key_list = jax.random.split(jax.random.key(seed), 8)
    part_keys = jax.random.split(jax.random.fold_in(key_list[7], part), 8)
    queries = draw_queries(jax.random.fold_in(jax.random.fold_in(key_list[7], part), 71), part)
    keys = draw_keys(jax.random.fold_in(jax.random.fold_in(key_list[7], part), 71), part)
    values = noise(part_keys[2], (SEQ, KVH * HD), 1.0, 6.0, ((0, 16), (1, 8)))
    block_order = jax.random.permutation(part_keys[3], BLOCKS).astype(jnp.int32)
    owner_of = draw_owner_of(jax.random.fold_in(jax.random.fold_in(key_list[7], part), 71), part)
    dec_queries = draw_dec_queries(jax.random.fold_in(jax.random.fold_in(key_list[7], part), 71), part)
    dec_pos = draw_dec_pos(jax.random.fold_in(jax.random.fold_in(key_list[7], part), 71), part)
    return {"queries": queries, "keys": keys, "values": values, "block_order": block_order, "owner_of": owner_of, "dec_queries": dec_queries, "dec_pos": dec_pos}


def row_positions(block_order):
    offsets = jnp.arange(BLK, dtype=jnp.int32)
    return (block_order.astype(jnp.int32)[:, None] * BLK + offsets[None, :]).reshape(SEQ)


def source_ranks(owner_of):
    ranks = jnp.arange(RANKS, dtype=jnp.int32)
    same = owner_of[None, :] == owner_of[:, None]
    earlier = ranks[None, :] < ranks[:, None]
    before = jnp.sum((same & earlier).astype(jnp.int32), axis=1)
    dest = owner_of.astype(jnp.int32) * (RANKS // OWNERS) + before
    hits = (dest[None, :] == ranks[:, None]).astype(jnp.int32)
    return jnp.sum(hits * ranks[None, :], axis=1).astype(jnp.int32)


def attend(query_rows, visible, keys, values):
    count = query_rows.shape[0]
    group = HQ // KVH
    query = query_rows.reshape(count, KVH, group, HD).astype(jnp.float32)
    key_all = keys.reshape(SEQ, KVH, HD).astype(jnp.float32)
    value_all = values.reshape(SEQ, KVH, HD).astype(jnp.float32)
    scores = jnp.einsum("rkgd,nkd->kgrn", query, key_all) * (HD ** -0.5)
    scores = jnp.where(visible, scores, -jnp.inf)
    top = jnp.max(scores, axis=3, keepdims=True)
    weights = jnp.where(visible, jnp.exp(scores - top), 0.0)
    total = jnp.sum(weights, axis=3)
    rounded = lax.optimization_barrier(weights.astype(jnp.bfloat16))
    mixed = jnp.einsum("kgrn,nkd->rkgd", rounded.astype(jnp.float32), value_all)
    mixed = mixed / jnp.transpose(total, (2, 0, 1))[..., None]
    return mixed.reshape(count, HQ * HD).astype(jnp.bfloat16)


def attend_blocks(query_rows, visible, keys, values):
    count = query_rows.shape[0]
    group = HQ // KVH
    query = query_rows.reshape(count, KVH, group, HD).astype(jnp.float32)
    key_all = keys.reshape(SEQ, KVH, HD).astype(jnp.float32)
    value_all = values.reshape(RANKS, TOK_DEV, KVH, HD).astype(jnp.float32)
    scores = jnp.einsum("rkgd,nkd->kgrn", query, key_all) * (HD ** -0.5)
    scores = jnp.where(visible, scores, -jnp.inf)
    top = jnp.max(scores, axis=3, keepdims=True)
    weights = jnp.where(visible, jnp.exp(scores - top), 0.0)
    weights = weights.reshape(KVH, group, count, RANKS, TOK_DEV)
    part_total = jnp.sum(weights, axis=4)
    rounded = lax.optimization_barrier(weights.astype(jnp.bfloat16))
    part_acc = jnp.einsum("kgrcn,cnkd->ckgrd", rounded.astype(jnp.float32), value_all)
    acc_bf = lax.optimization_barrier(part_acc.astype(jnp.bfloat16))
    total_bf = lax.optimization_barrier(part_total.astype(jnp.bfloat16))
    acc_sum = jnp.sum(acc_bf.astype(jnp.float32), axis=0)
    total_sum = jnp.sum(total_bf.astype(jnp.float32), axis=3)
    mixed = acc_sum / total_sum[..., None]
    mixed = jnp.transpose(mixed, (2, 0, 1, 3))
    return mixed.reshape(count, HQ * HD).astype(jnp.bfloat16)


def reference(queries, keys, values, block_order, owner_of, dec_queries, dec_pos):
    positions = row_positions(block_order)
    width = math.gcd(SEQ, 256)
    query_blocks = queries.reshape(SEQ // width, width, HQ * HD)
    place_blocks = positions.reshape(SEQ // width, width)

    def prefill(item):
        rows_here, place_here = item
        return attend(rows_here, place_here[:, None] >= positions[None, :], keys, values)

    attn_out = lax.map(prefill, (query_blocks, place_blocks)).reshape(SEQ, HQ * HD)
    source = source_ranks(owner_of)
    owned_keys = keys.reshape(RANKS, TOK_DEV, KVH * HD)[source].reshape(SEQ, KVH * HD)
    owned_values = values.reshape(RANKS, TOK_DEV, KVH * HD)[source].reshape(SEQ, KVH * HD)

    def decode(item):
        rows_here, limit = item
        return attend_blocks(rows_here, positions[None, :] < limit.astype(jnp.int32)[:, None], keys, values)

    dec_out = lax.map(decode, (dec_queries, dec_pos))
    return attn_out, owned_keys, owned_values, dec_out
```

```python
import functools

import jax
import jax.numpy as jnp
from jax import lax
from jax.experimental import pallas as pl
from jax.experimental.pallas import tpu as pltpu
from jax.sharding import PartitionSpec as P

HD = 128
BLK = 128
DROWS = 128
STEPS = 4
OWNERS = 4
HALVES = 2

LOWEST = -1e30
LOG2E = 1.4426950408889634
SCALE = LOG2E * HD ** (-0.5)
CHUNK = 512


def source_rank(owner_of, rank_here, ranks):
    index = jnp.arange(ranks, dtype=jnp.int32)
    same = owner_of[None, :] == owner_of[:, None]
    earlier = index[None, :] < index[:, None]
    before = jnp.sum((same & earlier).astype(jnp.int32), axis=1)
    dest = owner_of * (ranks // OWNERS) + before
    return jnp.sum(jnp.where(dest == rank_here, index, 0))


def attend(query, pairs, key_places, row_places, acc, total, top):
    count = pairs.shape[0]
    for first in range(0, count, CHUNK):
        width = min(CHUNK, count - first)
        key_rows = pairs[first : first + width, 0:HD]
        value_rows = pairs[first : first + width, HD : 2 * HD]
        places = key_places[:, first : first + width]
        scores = lax.dot_general(
            query, key_rows, (((1,), (1,)), ((), ())), preferred_element_type=jnp.float32
        )
        visible = jnp.tile(row_places, (1, width // HD)) >= places
        scores = jnp.where(visible, scores, LOWEST)
        new_top = jnp.maximum(top, jnp.max(scores, axis=1, keepdims=True))
        weights = jnp.exp2(scores * SCALE - jnp.tile(new_top * SCALE, (1, width // HD)))
        fade = jnp.exp2((top - new_top) * SCALE)
        wide = jnp.concatenate([value_rows, jnp.ones_like(value_rows)], axis=1)
        mixed = jnp.dot(weights.astype(jnp.bfloat16), wide, preferred_element_type=jnp.float32)
        acc = acc * fade + mixed[:, 0:HD]
        total = total * fade + mixed[:, HD : 2 * HD]
        top = new_top
    return acc, total, top


def group_query(group, heads, query_ref, dec_query_ref):
    return jnp.where(group < heads, query_ref[...], dec_query_ref[...])


def first_kernel(heads, query_ref, dec_query_ref, pairs_ref, key_places_ref, row_places_ref, state_ref):
    group = pl.program_id(0)
    query = group_query(group, heads, query_ref, dec_query_ref)
    rows = query.shape[0]
    acc = jnp.zeros((rows, HD), jnp.float32)
    top = jnp.full((rows, HD), LOWEST, jnp.float32)
    acc, total, top = attend(query, pairs_ref, key_places_ref[...], row_places_ref[0], acc, acc, top)
    lane = lax.broadcasted_iota(jnp.int32, (rows, HD), 1)
    state_ref[0, :, 0:HD] = acc
    state_ref[0, :, HD : 2 * HD] = jnp.where(lane < HD // 2, total, top)


def last_kernel(
    heads,
    pick_ref,
    query_ref,
    dec_query_ref,
    pairs_ref,
    key_places_ref,
    row_places_ref,
    state_ref,
    other_ref,
    out_ref,
    owned_keys_ref,
    owned_values_ref,
    dec_out_ref,
):
    group = pl.program_id(0)
    query = group_query(group, heads, query_ref, dec_query_ref)
    rows = query.shape[0]
    acc = state_ref[0, :, 0:HD]
    total = jnp.broadcast_to(state_ref[0, :, HD : HD + 1], (rows, HD))
    top = jnp.broadcast_to(state_ref[0, :, 2 * HD - 1 : 2 * HD], (rows, HD))
    acc, total, top = attend(query, pairs_ref, key_places_ref[...], row_places_ref[0], acc, total, top)
    mixed = (acc / total).astype(out_ref.dtype)

    @pl.when(group == 0)
    def _():
        here = pairs_ref[pl.ds(pl.multiple_of(pick_ref[1], rows), rows), :]
        picked = jnp.where(pick_ref[0] == 1, here, other_ref[...])
        owned_keys_ref[...] = picked[:, 0:HD]
        owned_values_ref[...] = picked[:, HD : 2 * HD]

    @pl.when(group < heads)
    def _():
        out_ref[...] = mixed

    @pl.when(group == heads)
    def _():
        steps, share = dec_out_ref.shape[0], dec_out_ref.shape[1]
        for head in range(heads):
            piece = mixed[head * steps * share : (head + 1) * steps * share]
            dec_out_ref[:, :, head * HD : (head + 1) * HD] = piece.reshape(steps, share, HD)


def per_device(queries, keys, values, block_order, owner_of, dec_queries, dec_pos):
    rows = queries.shape[0]
    heads = queries.shape[1] // HD
    groups = heads + 1
    ranks = lax.axis_size("ctx")
    rank_here = lax.axis_index("ctx")
    along = ranks // HALVES
    half_here = rank_here // along
    lines = [[half * along + place for place in range(along)] for half in range(HALVES)]
    swap = [(rank, (rank + along) % ranks) for rank in range(ranks)]
    share = DROWS // ranks

    pair = jnp.concatenate([keys, values], axis=1)
    near = lax.all_gather(pair, "ctx", axis=0, axis_index_groups=lines, tiled=True)
    partner = lax.ppermute(pair, "ctx", swap)
    copies = jnp.broadcast_to(partner[None], (along,) + partner.shape)
    far = lax.all_to_all(copies, "ctx", 0, 0, axis_index_groups=lines)
    far = far.reshape(along * rows, 2 * HD)

    places = (block_order[:, None] * BLK + jnp.arange(BLK, dtype=jnp.int32)[None, :]).reshape(1, -1)
    span = along * rows
    near_places = lax.dynamic_slice_in_dim(places, half_here * span, span, 1)
    far_places = lax.dynamic_slice_in_dim(places, (1 - half_here) * span, span, 1)
    query_places = lax.dynamic_slice_in_dim(places, rank_here * rows, rows, 1).reshape(rows)
    dec_mine = lax.dynamic_slice_in_dim(dec_queries, rank_here * share, share, 1)
    dec_query = jnp.transpose(dec_mine.reshape(STEPS * share, heads, HD), (1, 0, 2)).reshape(-1, HD)
    limits = lax.dynamic_slice_in_dim(dec_pos, rank_here * share, share, 1).reshape(-1)
    dec_places = jnp.tile(limits - 1, (heads,))
    row_places = jnp.stack([query_places, dec_places])
    row_places = jnp.broadcast_to(row_places[:, :, None], (2, rows, HD))

    source = source_rank(owner_of, rank_here, ranks)
    source_near = source // along == half_here
    offset = (source % along) * rows
    other = lax.dynamic_slice_in_dim(far, offset, rows, 0)
    pick = jnp.stack([source_near.astype(jnp.int32), offset])

    whole = lambda *shape: pl.BlockSpec(shape, lambda group, *_: (0,) * len(shape))
    query_spec = pl.BlockSpec((rows, HD), lambda group, *_: (0, jnp.minimum(group, heads - 1)))
    places_spec = pl.BlockSpec((1, rows, HD), lambda group, *_: (group // heads, 0, 0))
    state_spec = pl.BlockSpec((1, rows, 2 * HD), lambda group, *_: (group, 0, 0))
    params = pltpu.CompilerParams(vmem_limit_bytes=48 * 2**20)
    inputs = [query_spec, whole(rows, HD), whole(span, 2 * HD), whole(1, span), places_spec]
    cost = pl.CostEstimate(
        flops=4 * groups * rows * span * HD,
        bytes_accessed=groups * rows * HD * 12 + span * HD * 4,
        transcendentals=groups * rows * span,
    )
    state = pl.pallas_call(
        functools.partial(first_kernel, heads),
        grid=(groups,),
        in_specs=inputs,
        out_specs=state_spec,
        out_shape=jax.ShapeDtypeStruct((groups, rows, 2 * HD), jnp.float32),
        compiler_params=params,
        cost_estimate=cost,
        name="attend_far",
    )(queries, dec_query, far, far_places, row_places)
    return pl.pallas_call(
        functools.partial(last_kernel, heads),
        grid_spec=pltpu.PrefetchScalarGridSpec(
            num_scalar_prefetch=1,
            grid=(groups,),
            in_specs=inputs + [state_spec, whole(rows, 2 * HD)],
            out_specs=[
                query_spec,
                whole(rows, HD),
                whole(rows, HD),
                whole(STEPS, share, heads * HD),
            ],
        ),
        out_shape=[
            jax.ShapeDtypeStruct(queries.shape, queries.dtype),
            jax.ShapeDtypeStruct(keys.shape, keys.dtype),
            jax.ShapeDtypeStruct(values.shape, values.dtype),
            jax.ShapeDtypeStruct((STEPS, share, heads * HD), queries.dtype),
        ],
        compiler_params=params,
        cost_estimate=cost,
        name="attend_near",
    )(pick, queries, dec_query, near, near_places, row_places, state, other)


def solution(mesh):
    placed = (
        P(("req", "ctx"), "head"),
        P(("req", "ctx"), "head"),
        P(("req", "ctx"), "head"),
        P("req"),
        P("req"),
        P("req", None, "head"),
        P("req", None),
    )
    return jax.shard_map(
        per_device,
        mesh=mesh,
        in_specs=placed,
        out_specs=(
            P(("req", "ctx"), "head"),
            P(("req", "ctx"), "head"),
            P(("req", "ctx"), "head"),
            P("req", "ctx", "head"),
        ),
        check_vma=False,
    )
```

```python
import functools

import jax
import jax.numpy as jnp
from jax import lax
from jax.experimental import pallas as pl
from jax.experimental.pallas import tpu as pltpu
from jax.sharding import PartitionSpec as P

HD = 128
BLK = 128
DROWS = 128
STEPS = 4
OWNERS = 4
HALVES = 2

LOWEST = -1e30
LOG2E = 1.4426950408889634
SCALE = LOG2E * HD ** (-0.5)


def source_rank(owner_of, rank_here, ranks):
    index = jnp.arange(ranks, dtype=jnp.int32)
    same = owner_of[None, :] == owner_of[:, None]
    earlier = index[None, :] < index[:, None]
    before = jnp.sum((same & earlier).astype(jnp.int32), axis=1)
    dest = owner_of * (ranks // OWNERS) + before
    return jnp.sum(jnp.where(dest == rank_here, index, 0))


def attend(order_ref, plan_ref, query_ref, dec_query_ref, limits_ref, pairs_refs, first_item, state):
    rows = query_ref.shape[0]
    heads = query_ref.shape[1] // HD
    lane = lax.broadcasted_iota(jnp.int32, (1, rows), 1)
    line = lax.broadcasted_iota(jnp.int32, (rows, HD), 0)

    def places(rank, index):
        low = order_ref[rank * 2] * BLK
        high = order_ref[rank * 2 + 1] * BLK - BLK
        return jnp.where(index < BLK, low, high) + index

    query_places = places(plan_ref[0], line)
    items = []
    for ref in pairs_refs:
        for start in range(0, ref.shape[0], 2 * rows):
            items.append((ref, start, places(plan_ref[1 + first_item + len(items)], lane)))
    for group in range(heads + 1):
        if group < heads:
            query = query_ref[:, group * HD : (group + 1) * HD]
            row_places = query_places
        else:
            query = dec_query_ref[...]
            row_places = limits_ref[...] - 1
        row_places = jnp.tile(row_places, (1, rows // HD))
        acc, total, top = state(group)
        for ref, start, key_places in items:
            key_rows = ref[start : start + rows, :]
            value_rows = ref[start + rows : start + 2 * rows, :]
            scores = lax.dot_general(
                query, key_rows, (((1,), (1,)), ((), ())), preferred_element_type=jnp.float32
            )
            scores = jnp.where(row_places >= key_places, scores, LOWEST)
            new_top = jnp.maximum(top, jnp.max(scores, axis=1, keepdims=True))
            weights = jnp.exp2(scores * SCALE - jnp.tile(new_top * SCALE, (1, rows // HD)))
            fade = jnp.exp2((top - new_top) * SCALE)
            wide = jnp.concatenate([value_rows, jnp.ones_like(value_rows)], axis=1)
            mixed = jnp.dot(
                weights.astype(jnp.bfloat16), wide, preferred_element_type=jnp.float32
            )
            acc = acc * fade + mixed[:, 0:HD]
            total = total * fade + mixed[:, HD : 2 * HD]
            top = new_top
        yield group, acc, total, top


def empty_state(rows):
    def state(group):
        zero = jnp.zeros((rows, HD), jnp.float32)
        return zero, zero, jnp.full((rows, HD), LOWEST, jnp.float32)

    return state


def held_state(state_ref):
    def state(group):
        return tuple(state_ref[group, :, part * HD : (part + 1) * HD] for part in range(3))

    return state


def first_kernel(order_ref, plan_ref, query_ref, dec_query_ref, limits_ref, pairs_ref, state_ref):
    state = empty_state(query_ref.shape[0])
    refs = (order_ref, plan_ref, query_ref, dec_query_ref, limits_ref, (pairs_ref,))
    for group, *parts in attend(*refs, 0, state):
        for part, value in enumerate(parts):
            state_ref[group, :, part * HD : (part + 1) * HD] = value


def next_kernel(
    first_item, order_ref, plan_ref, query_ref, dec_query_ref, limits_ref, right_ref, left_ref, held_ref, state_ref
):
    state = held_state(held_ref)
    refs = (order_ref, plan_ref, query_ref, dec_query_ref, limits_ref, (right_ref, left_ref))
    for group, *parts in attend(*refs, first_item, state):
        for part, value in enumerate(parts):
            state_ref[group, :, part * HD : (part + 1) * HD] = value


def last_kernel(
    first_item,
    places,
    order_ref,
    plan_ref,
    pick_ref,
    query_ref,
    dec_query_ref,
    limits_ref,
    pairs_ref,
    held_ref,
    *rest,
):
    sources = rest[:places]
    out_ref, owned_keys_ref, owned_values_ref, dec_out_ref, out_rows, dec_rows, out_sems, owned_sems, dec_sem = rest[
        places:
    ]
    rows = query_ref.shape[0]
    heads = query_ref.shape[1] // HD
    steps, share = dec_out_ref.shape[0], dec_out_ref.shape[1]

    def hand_over(source, offset):
        keys = source.at[pl.ds(offset, rows), :]
        values = source.at[pl.ds(offset + rows, rows), :]
        return (
            pltpu.make_async_copy(keys, owned_keys_ref, owned_sems.at[0]),
            pltpu.make_async_copy(values, owned_values_ref, owned_sems.at[1]),
        )

    for place, source in enumerate(sources):

        @pl.when(pick_ref[0] == place)
        def _(source=source):
            for copy in hand_over(source, pl.multiple_of(pick_ref[1], rows)):
                copy.start()

    copies = []
    refs = (order_ref, plan_ref, query_ref, dec_query_ref, limits_ref, (pairs_ref,))
    for group, acc, total, _ in attend(*refs, first_item, held_state(held_ref)):
        mixed = (acc / total).astype(jnp.bfloat16)
        if group < heads:
            across = pl.ds(group * HD, HD)
            out_rows[group] = mixed
            copies.append(pltpu.make_async_copy(out_rows.at[group], out_ref.at[:, across], out_sems.at[group]))
        else:
            for head in range(heads):
                piece = mixed[head * steps * share : (head + 1) * steps * share]
                dec_rows[:, :, head * HD : (head + 1) * HD] = piece.reshape(steps, share, HD)
            copies.append(pltpu.make_async_copy(dec_rows, dec_out_ref, dec_sem))
        copies[-1].start()
    for copy in copies:
        copy.wait()
    for copy in hand_over(sources[0], 0):
        copy.wait()


def per_device(queries, keys, values, block_order, owner_of, dec_queries, dec_pos):
    rows = queries.shape[0]
    heads = queries.shape[1] // HD
    groups = heads + 1
    ranks = lax.axis_size("ctx")
    rank_here = lax.axis_index("ctx")
    along = ranks // HALVES
    share = DROWS // ranks
    place_here = rank_here % along

    def shift(block, by):
        moves = []
        for rank in range(ranks):
            half, place = rank // along, rank % along
            moves.append((rank, half * along + (place + by) % along))
        return lax.ppermute(block, "ctx", moves)

    across = [[half * along + place for half in range(HALVES)] for place in range(along)]
    pair = jnp.concatenate([keys, values], axis=0)
    here = lax.all_gather(pair, "ctx", axis=0, axis_index_groups=across, tiled=True)
    rights, lefts = [here], [here]
    for step in range(1, along // 2):
        rights.append(shift(rights[-1], -1))
        lefts.append(shift(lefts[-1], 1))
    opposite = shift(rights[-1], -1)

    dec_mine = lax.dynamic_slice_in_dim(dec_queries, rank_here * share, share, 1)
    dec_query = jnp.transpose(dec_mine.reshape(STEPS * share, heads, HD), (1, 0, 2)).reshape(-1, HD)
    limits = lax.dynamic_slice_in_dim(dec_pos, rank_here * share, share, 1).reshape(-1)
    limits = jnp.broadcast_to(jnp.tile(limits, (heads,))[:, None], (rows, HD))

    distances = [0]
    for step in range(1, along // 2):
        distances += [step, -step]
    distances.append(along // 2)
    held_at = [(place_here + distance) % along for distance in distances]
    plan = [rank_here] + [half * along + place for place in held_at for half in range(HALVES)]
    plan = jnp.stack(plan).astype(jnp.int32)

    source = source_rank(owner_of, rank_here, ranks)
    found = jnp.stack(held_at) == source % along
    pick = jnp.stack([jnp.argmax(found).astype(jnp.int32), (source // along) * 2 * rows])

    smem = pl.BlockSpec(memory_space=pltpu.SMEM)
    vmem = pl.BlockSpec(memory_space=pltpu.VMEM)
    anywhere = pl.BlockSpec(memory_space=pl.ANY)
    state_shape = jax.ShapeDtypeStruct((groups, rows, 3 * HD), jnp.float32)
    fixed = (queries, dec_query, limits)

    def cost(items):
        return pl.CostEstimate(
            flops=8 * groups * rows * items * rows * HD,
            bytes_accessed=items * rows * HD * 4,
            transcendentals=groups * rows * items * rows,
        )

    params = pltpu.CompilerParams(vmem_limit_bytes=24 * 2**20)
    state = pl.pallas_call(
        first_kernel,
        in_specs=[smem] * 2 + [vmem] * 4,
        out_specs=vmem,
        out_shape=state_shape,
        compiler_params=params,
        cost_estimate=cost(HALVES),
        name="attend_here",
    )(block_order, plan, *fixed, here)
    for step in range(1, along // 2):
        state = pl.pallas_call(
            functools.partial(next_kernel, HALVES * (2 * step - 1)),
            in_specs=[smem] * 2 + [vmem] * 6,
            out_specs=vmem,
            out_shape=state_shape,
            compiler_params=params,
            cost_estimate=cost(2 * HALVES),
            name=f"attend_{step}",
        )(block_order, plan, *fixed, rights[step], lefts[step], state)
    sources = [here]
    for step in range(1, along // 2):
        sources += [rights[step], lefts[step]]
    sources.append(opposite)
    return pl.pallas_call(
        functools.partial(last_kernel, HALVES * (along - 1), len(sources)),
        in_specs=[smem] * 3 + [vmem] * 5 + [anywhere] * len(sources),
        out_specs=[anywhere] * 4,
        out_shape=[
            jax.ShapeDtypeStruct(queries.shape, queries.dtype),
            jax.ShapeDtypeStruct(keys.shape, keys.dtype),
            jax.ShapeDtypeStruct(values.shape, values.dtype),
            jax.ShapeDtypeStruct((STEPS, share, heads * HD), queries.dtype),
        ],
        scratch_shapes=[
            pltpu.VMEM((heads, rows, HD), jnp.bfloat16),
            pltpu.VMEM((STEPS, share, heads * HD), jnp.bfloat16),
            pltpu.SemaphoreType.DMA((heads,)),
            pltpu.SemaphoreType.DMA((2,)),
            pltpu.SemaphoreType.DMA(()),
        ],
        compiler_params=params,
        cost_estimate=cost(HALVES),
        name="attend_last",
    )(block_order, plan, pick, *fixed, opposite, state, *sources)


def solution(mesh):
    placed = (
        P(("req", "ctx"), "head"),
        P(("req", "ctx"), "head"),
        P(("req", "ctx"), "head"),
        P("req"),
        P("req"),
        P("req", None, "head"),
        P("req", None),
    )
    return jax.shard_map(
        per_device,
        mesh=mesh,
        in_specs=placed,
        out_specs=(
            P(("req", "ctx"), "head"),
            P(("req", "ctx"), "head"),
            P(("req", "ctx"), "head"),
            P("req", "ctx", "head"),
        ),
        check_vma=False,
    )
```

```python
import functools

import jax
import jax.numpy as jnp
from jax import lax
from jax.experimental import pallas as pl
from jax.experimental.pallas import tpu as pltpu
from jax.sharding import PartitionSpec as P

HD = 128
BLK = 128
DROWS = 128
STEPS = 4
OWNERS = 4
HALVES = 2
TILE = 16
TOGETHER = 2

LOWEST = -1e30
LOG2E = 1.4426950408889634
SCALE = LOG2E * HD ** (-0.5)
REACH = 64.0


def largest_norm(rows):
    lengths = jnp.sum(rows * rows, axis=1, keepdims=True)
    return jnp.max(lengths, axis=0, keepdims=True)


def attend(refs, pairs_refs, places_of, along, calm, was_calm, sums_ref, tops_ref, emit, settle=lambda: None):
    here_ref, order_ref, query_ref, dec_query_ref, limits_ref = refs
    rows, heads = query_ref.shape[0], query_ref.shape[1] // HD
    groups = heads + 1
    here = here_ref[0]
    lane = lax.broadcasted_iota(jnp.int32, (1, rows), 1)
    line = lax.broadcasted_iota(jnp.int32, (rows, HD), 0)

    def places(rank, index):
        low = order_ref[rank * 2] * BLK
        high = order_ref[rank * 2 + 1] * BLK - BLK
        return jnp.where(index < BLK, low, high) + index

    query_places = places(here, line)
    dec_places = jnp.tile(limits_ref[...] - 1, (heads, 1))
    blocks = [(ref, start) for ref in pairs_refs for start in range(0, ref.shape[0], 2 * rows)]
    items = []
    for (ref, start), (distance, other) in zip(blocks, places_of):
        half = here // along
        half = 1 - half if other else half
        rank = half * along + lax.rem(here + distance + along, along)
        items.append((ref, start, places(rank, lane)))

    def item_rows(part):
        keys = [ref[start : start + rows, :] for ref, start, _ in part]
        values = [ref[start + rows : start + 2 * rows, :] for ref, start, _ in part]
        wide = [jnp.concatenate([value, jnp.ones_like(value)], axis=1) for value in values]
        return jnp.concatenate(keys, axis=0), jnp.concatenate(wide, axis=0)

    def masked(query, keys, part, row_places):
        scores = lax.dot_general(query, keys, (((1,), (1,)), ((), ())), preferred_element_type=jnp.float32)
        key_places = jnp.concatenate([key_places for _, _, key_places in part], axis=1)
        visible = jnp.tile(row_places, (1, key_places.shape[1] // HD)) >= key_places
        return jnp.where(visible, scores * SCALE, LOWEST)

    parts = [items[first : first + TOGETHER] for first in range(0, len(items), TOGETHER)]

    def start_sums(group):
        return jnp.zeros((rows, 2 * HD), jnp.float32) if sums_ref is None else sums_ref[group]

    for group in range(groups):
        row_places = query_places if group < heads else dec_places
        query = query_ref[:, group * HD : (group + 1) * HD] if group < heads else dec_query_ref[...]
        sums = start_sums(group)
        for part in parts:
            keys, wide = item_rows(part)
            weights = jnp.exp2(masked(query, keys, part, row_places))
            sums += jnp.dot(weights.astype(jnp.bfloat16), wide, preferred_element_type=jnp.float32)
        emit(group, sums, None)

    @pl.when(jnp.logical_not(calm))
    def _():
        settle()

        def visit(group, _):
            row_places = jnp.where(group < heads, query_places, dec_places)
            across = pl.ds(pl.multiple_of(jnp.minimum(group, heads - 1) * HD, HD), HD)
            query = jnp.where(group < heads, query_ref[:, across], dec_query_ref[...])
            sums = start_sums(group)
            top = jnp.where(sums[:, HD:] > 0.0, 0.0, LOWEST)
            if tops_ref is not None:
                top = jnp.where(was_calm, top, tops_ref[group])
            for part in parts:
                keys, wide = item_rows(part)
                scores = masked(query, keys, part, row_places)
                new_top = jnp.maximum(top, jnp.max(scores, axis=1, keepdims=True))
                weights = jnp.exp2(scores - jnp.tile(new_top, (1, scores.shape[1] // HD)))
                fade = jnp.tile(jnp.exp2(top - new_top), (1, 2))
                sums = sums * fade + jnp.dot(
                    weights.astype(jnp.bfloat16), wide, preferred_element_type=jnp.float32
                )
                top = new_top
            emit(group, sums, top)
            return 0

        lax.fori_loop(0, groups, visit, 0)


def reach_of(query_norm, key_norm):
    return jnp.max(query_norm * key_norm)


def key_norms(pairs_refs, rows):
    norm = None
    for ref in pairs_refs:
        for start in range(0, ref.shape[0], 2 * rows):
            found = largest_norm(ref[start : start + rows, :].astype(jnp.float32))
            norm = found if norm is None else jnp.maximum(norm, found)
    return norm


def first_kernel(
    along, here_ref, order_ref, limit_ref, query_ref, dec_ref, pairs_ref, dec_query_ref, limits_ref, norms_ref, sums_ref, tops_ref, dec_rows
):
    rows, heads = query_ref.shape[0], query_ref.shape[1] // HD
    steps, share = dec_ref.shape[0], limits_ref.shape[0] // dec_ref.shape[0]
    first = here_ref[0] * share
    base = pl.multiple_of(first // TILE * TILE, TILE)
    for head in range(heads):
        for step in range(steps):
            block = dec_ref[step, pl.ds(base, TILE), head * HD : (head + 1) * HD].astype(jnp.float32)
            mine = block[0:share]
            for other in range(share, TILE, share):
                mine = jnp.where(first - base == other, block[other : other + share], mine)
            dec_rows[(head * steps + step) * share : (head * steps + step + 1) * share, :] = mine
    for step in range(steps):
        for row in range(share):
            limits_ref[step * share + row : step * share + row + 1, :] = jnp.full(
                (1, HD), limit_ref[step, first + row], jnp.int32
            )
    dec_query_ref[...] = dec_rows[...].astype(jnp.bfloat16)
    query_norm = largest_norm(dec_rows[...])
    for head in range(heads):
        query = query_ref[:, head * HD : (head + 1) * HD].astype(jnp.float32)
        query_norm = jnp.maximum(query_norm, largest_norm(query))
    query_norm = query_norm * (SCALE * SCALE)
    key_norm = key_norms((pairs_ref,), rows)
    norms_ref[0] = jnp.broadcast_to(query_norm, norms_ref.shape[1:])
    norms_ref[1] = jnp.broadcast_to(key_norm, norms_ref.shape[1:])
    calm = reach_of(query_norm, key_norm) <= REACH * REACH

    def emit(group, sums, top):
        sums_ref[group] = sums
        if top is not None:
            tops_ref[group] = top

    refs = (here_ref, order_ref, query_ref, dec_query_ref, limits_ref)
    attend(refs, (pairs_ref,), ((0, False),), along, calm, True, None, None, emit)


def norms_so_far(norms_ref, pairs_refs, rows):
    query_norm, before = norms_ref[0], norms_ref[1]
    now = jnp.maximum(before, key_norms(pairs_refs, rows))
    bound = REACH * REACH
    return now, reach_of(query_norm, now) <= bound, reach_of(query_norm, before) <= bound


def next_kernel(along, places_of, blocks, here_ref, order_ref, query_ref, dec_query_ref, limits_ref, norms_in, sums_in, tops_in, *rest):
    pairs_refs = rest[:blocks]
    norms_ref, sums_ref, tops_ref = rest[blocks:]
    now, calm, was_calm = norms_so_far(norms_in, pairs_refs, query_ref.shape[0])
    norms_ref[0] = norms_in[0]
    norms_ref[1] = now

    def emit(group, sums, top):
        sums_ref[group] = sums
        if top is not None:
            tops_ref[group] = top

    refs = (here_ref, order_ref, query_ref, dec_query_ref, limits_ref)
    attend(refs, pairs_refs, places_of, along, calm, was_calm, sums_in, tops_in, emit)


def last_kernel(along, places_of, taken, arrivals, here_ref, order_ref, owner_ref, query_ref, dec_query_ref, limits_ref, norms_in, sums_in, tops_in, *rest):
    pairs_refs, rest = rest[:taken], rest[taken:]
    places = len(arrivals)
    sources = rest[:places]
    (out_ref, owned_keys_ref, owned_values_ref, dec_out_ref, out_rows, dec_rows, out_sems, owned_sems, dec_sem) = rest[places:]
    rows, heads = query_ref.shape[0], query_ref.shape[1] // HD
    steps, share = dec_out_ref.shape[0], dec_out_ref.shape[1]
    here = here_ref[0]

    ranks = owner_ref.shape[0]
    slots = ranks // OWNERS
    owner, turn = here // slots, here % slots
    source, seen = jnp.int32(0), jnp.int32(0)
    for rank in range(ranks):
        match = owner_ref[rank] == owner
        source = jnp.where(jnp.logical_and(match, seen == turn), rank, source)
        seen = seen + match.astype(jnp.int32)
    offset = pl.multiple_of(jnp.where(source // along == here // along, 0, 2 * rows), 2 * rows)
    apart = lax.rem(source - here + 2 * along, along)

    def hand_over(block, start):
        return (
            pltpu.make_async_copy(block.at[pl.ds(start, rows), :], owned_keys_ref, owned_sems.at[0]),
            pltpu.make_async_copy(block.at[pl.ds(start + rows, rows), :], owned_values_ref, owned_sems.at[1]),
        )

    for block, distance in zip(sources, arrivals):

        @pl.when(apart == distance % along)
        def _(block=block):
            for copy in hand_over(block, offset):
                copy.start()

    def emit_head(group, mixed):
        out_rows[group] = mixed
        out_copy(group).start()

    def emit_decode(mixed):
        for head in range(heads):
            piece = mixed[head * steps * share : (head + 1) * steps * share]
            dec_rows[:, :, head * HD : (head + 1) * HD] = piece.reshape(steps, share, HD)
        dec_copy.start()

    def out_copy(group):
        across = pl.ds(pl.multiple_of(group * HD, HD), HD)
        return pltpu.make_async_copy(out_rows.at[group], out_ref.at[:, across], out_sems.at[group])

    dec_copy = pltpu.make_async_copy(dec_rows, dec_out_ref, dec_sem)

    def emit(group, sums, top):
        mixed = (sums[:, 0:HD] / sums[:, HD:]).astype(jnp.bfloat16)
        if top is None:
            emit_head(group, mixed) if group < heads else emit_decode(mixed)
        else:
            pl.when(group < heads)(lambda: emit_head(group, mixed))
            pl.when(group == heads)(lambda: emit_decode(mixed))

    def settle():
        for group in range(heads):
            out_copy(group).wait()
        dec_copy.wait()

    _, calm, was_calm = norms_so_far(norms_in, pairs_refs, rows)
    refs = (here_ref, order_ref, query_ref, dec_query_ref, limits_ref)
    attend(refs, pairs_refs, places_of, along, calm, was_calm, sums_in, tops_in, emit, settle)
    settle()
    for copy in hand_over(sources[0], 0):
        copy.wait()


def pack_kernel(keys_ref, values_ref, pair_ref, sems):
    rows = keys_ref.shape[0]
    copies = (
        pltpu.make_async_copy(keys_ref, pair_ref.at[0:rows], sems.at[0]),
        pltpu.make_async_copy(values_ref, pair_ref.at[rows : 2 * rows], sems.at[1]),
    )
    for copy in copies:
        copy.start()
    for copy in copies:
        copy.wait()


def per_device(queries, keys, values, block_order, owner_of, dec_queries, dec_pos):
    rows = queries.shape[0]
    heads = queries.shape[1] // HD
    groups = heads + 1
    ranks = lax.axis_size("ctx")
    here = lax.axis_index("ctx").astype(jnp.int32).reshape(1)
    along = ranks // HALVES
    share = DROWS // ranks

    def shift(block, by):
        moves = []
        for rank in range(ranks):
            half, place = rank // along, rank % along
            moves.append((rank, half * along + (place + by) % along))
        return lax.ppermute(block, "ctx", moves)

    swap = [(rank, (rank + along) % ranks) for rank in range(ranks)]
    own = pl.pallas_call(
        pack_kernel,
        in_specs=[pl.BlockSpec(memory_space=pl.ANY)] * 2,
        out_specs=pl.BlockSpec(memory_space=pltpu.VMEM),
        out_shape=jax.ShapeDtypeStruct((2 * rows, HD), keys.dtype),
        scratch_shapes=[pltpu.SemaphoreType.DMA((2,))],
        name="pack",
    )(keys, values)
    other = lax.ppermute(own, "ctx", swap)
    local = jnp.concatenate([own, other], axis=0)
    rights, lefts = [local], [local]
    for step in range(1, along // 2):
        rights.append(shift(rights[-1], -1))
        lefts.append(shift(lefts[-1], 1))
    rounds = [{step: rights[step], -step: lefts[step]} for step in range(1, along // 2)]
    last = {along // 2: shift(rights[-1], -1)}

    smem = pl.BlockSpec(memory_space=pltpu.SMEM)
    vmem = pl.BlockSpec(memory_space=pltpu.VMEM)
    anywhere = pl.BlockSpec(memory_space=pl.ANY)
    shape = jax.ShapeDtypeStruct
    carried = [
        shape((2, 8, HD), jnp.float32),
        shape((groups, rows, 2 * HD), jnp.float32),
        shape((groups, rows, HD), jnp.float32),
    ]

    def cost(items):
        return pl.CostEstimate(
            flops=4 * 8 * groups * rows * items * rows * HD,
            bytes_accessed=items * rows * HD * 4,
            transcendentals=groups * rows * items * rows,
        )

    params = pltpu.CompilerParams(vmem_limit_bytes=24 * 2**20)
    dec_query, limits, *state = pl.pallas_call(
        functools.partial(first_kernel, along),
        in_specs=[smem] * 3 + [vmem] * 3,
        out_specs=[vmem] * 5,
        out_shape=[shape((rows, HD), jnp.bfloat16), shape((STEPS * share, HD), jnp.int32)] + carried,
        scratch_shapes=[pltpu.VMEM((rows, HD), jnp.float32)],
        compiler_params=params,
        cost_estimate=cost(1),
        name="attend_own",
    )(here, block_order, dec_pos, queries, dec_queries, own)
    fixed = (queries, dec_query, limits)

    def attend_more(state, blocks, places_of, name):
        return pl.pallas_call(
            functools.partial(next_kernel, along, places_of, len(blocks)),
            in_specs=[smem] * 2 + [vmem] * (6 + len(blocks)),
            out_specs=[vmem] * 3,
            out_shape=carried,
            compiler_params=params,
            cost_estimate=cost(max(len(places_of), 2 * HALVES)),
            name=name,
        )(here, block_order, *fixed, *state, *blocks)

    state = attend_more(state, [other], ((0, True),), "attend_other")
    def halves_of(blocks):
        return tuple((distance, other) for distance in blocks for other in (False, True))

    for number, blocks in enumerate(rounds):
        state = attend_more(state, list(blocks.values()), halves_of(blocks), f"attend_{number}")
    sources = {0: local}
    for blocks in rounds + [last]:
        sources.update(blocks)
    return pl.pallas_call(
        functools.partial(last_kernel, along, halves_of(last), len(last), tuple(sources)),
        in_specs=[smem] * 3 + [vmem] * (6 + len(last)) + [anywhere] * len(sources),
        out_specs=[anywhere] * 4,
        out_shape=[
            shape(queries.shape, queries.dtype),
            shape(keys.shape, keys.dtype),
            shape(values.shape, values.dtype),
            shape((STEPS, share, heads * HD), queries.dtype),
        ],
        scratch_shapes=[
            pltpu.VMEM((heads, rows, HD), jnp.bfloat16),
            pltpu.VMEM((STEPS, share, heads * HD), jnp.bfloat16),
            pltpu.SemaphoreType.DMA((heads,)),
            pltpu.SemaphoreType.DMA((2,)),
            pltpu.SemaphoreType.DMA(()),
        ],
        compiler_params=params,
        cost_estimate=cost(HALVES),
        name="attend_last",
    )(here, block_order, owner_of, *fixed, *state, *last.values(), *sources.values())


def solution(mesh):
    placed = (
        P(("req", "ctx"), "head"),
        P(("req", "ctx"), "head"),
        P(("req", "ctx"), "head"),
        P("req"),
        P("req"),
        P("req", None, "head"),
        P("req", None),
    )
    return jax.shard_map(
        per_device,
        mesh=mesh,
        in_specs=placed,
        out_specs=(
            P(("req", "ctx"), "head"),
            P(("req", "ctx"), "head"),
            P(("req", "ctx"), "head"),
            P("req", "ctx", "head"),
        ),
        check_vma=False,
    )
```

```python
import functools

import jax
import jax.numpy as jnp
from jax import lax
from jax.experimental import pallas as pl
from jax.experimental.pallas import tpu as pltpu
from jax.sharding import PartitionSpec as P

HD = 128
BLK = 128
DROWS = 128
STEPS = 4
OWNERS = 4
HALVES = 2
TILE = 16
TOGETHER = 2

LOWEST = -1e30
LOG2E = 1.4426950408889634
SCALE = LOG2E * HD ** (-0.5)
REACH = 64.0


def largest_norm(rows):
    lengths = jnp.sum(rows * rows, axis=1, keepdims=True)
    return jnp.max(lengths, axis=0, keepdims=True)


def attend(refs, pairs_refs, places_of, along, calm, was_calm, sums_ref, tops_ref, emit, settle=lambda: None):
    here_ref, order_ref, query_ref, dec_query_ref, limits_ref = refs
    rows, heads = query_ref.shape[0], query_ref.shape[1] // HD
    groups = heads + 1
    here = here_ref[0]
    lane = lax.broadcasted_iota(jnp.int32, (1, rows), 1)
    line = lax.broadcasted_iota(jnp.int32, (rows, HD), 0)

    def places(rank, index):
        low = order_ref[rank * 2] * BLK
        high = order_ref[rank * 2 + 1] * BLK - BLK
        return jnp.where(index < BLK, low, high) + index

    query_places = places(here, line)
    dec_places = jnp.tile(limits_ref[...] - 1, (heads, 1))
    blocks = [(ref, start) for ref in pairs_refs for start in range(0, ref.shape[0], 2 * rows)]
    items = []
    for (ref, start), (distance, other) in zip(blocks, places_of):
        half = here // along
        half = 1 - half if other else half
        rank = half * along + lax.rem(here + distance + along, along)
        items.append((ref, start, places(rank, lane)))

    def item_rows(part):
        keys = [ref[start : start + rows, :] for ref, start, _ in part]
        values = [ref[start + rows : start + 2 * rows, :] for ref, start, _ in part]
        wide = [jnp.concatenate([value, jnp.ones_like(value)], axis=1) for value in values]
        return jnp.concatenate(keys, axis=0), jnp.concatenate(wide, axis=0)

    def masked(query, keys, part, row_places):
        scores = lax.dot_general(query, keys, (((1,), (1,)), ((), ())), preferred_element_type=jnp.float32)
        key_places = jnp.concatenate([key_places for _, _, key_places in part], axis=1)
        visible = jnp.tile(row_places, (1, key_places.shape[1] // HD)) >= key_places
        return jnp.where(visible, scores * SCALE, LOWEST)

    parts = [items[first : first + TOGETHER] for first in range(0, len(items), TOGETHER)]

    def start_sums(group):
        return jnp.zeros((rows, 2 * HD), jnp.float32) if sums_ref is None else sums_ref[group]

    for group in range(groups):
        row_places = query_places if group < heads else dec_places
        query = query_ref[:, group * HD : (group + 1) * HD] if group < heads else dec_query_ref[...]
        sums = start_sums(group)
        for part in parts:
            keys, wide = item_rows(part)
            weights = jnp.exp2(masked(query, keys, part, row_places))
            sums += jnp.dot(weights.astype(jnp.bfloat16), wide, preferred_element_type=jnp.float32)
        emit(group, sums, None)

    @pl.when(jnp.logical_not(calm))
    def _():
        settle()

        def visit(group, _):
            row_places = jnp.where(group < heads, query_places, dec_places)
            across = pl.ds(pl.multiple_of(jnp.minimum(group, heads - 1) * HD, HD), HD)
            query = jnp.where(group < heads, query_ref[:, across], dec_query_ref[...])
            sums = start_sums(group)
            top = jnp.where(sums[:, HD:] > 0.0, 0.0, LOWEST)
            if tops_ref is not None:
                top = jnp.where(was_calm, top, tops_ref[group])
            for part in parts:
                keys, wide = item_rows(part)
                scores = masked(query, keys, part, row_places)
                new_top = jnp.maximum(top, jnp.max(scores, axis=1, keepdims=True))
                weights = jnp.exp2(scores - jnp.tile(new_top, (1, scores.shape[1] // HD)))
                fade = jnp.tile(jnp.exp2(top - new_top), (1, 2))
                sums = sums * fade + jnp.dot(
                    weights.astype(jnp.bfloat16), wide, preferred_element_type=jnp.float32
                )
                top = new_top
            emit(group, sums, top)
            return 0

        lax.fori_loop(0, groups, visit, 0)


def reach_of(query_norm, key_norm):
    return jnp.max(query_norm * key_norm)


def key_norms(pairs_refs, rows):
    norm = None
    for ref in pairs_refs:
        for start in range(0, ref.shape[0], 2 * rows):
            found = largest_norm(ref[start : start + rows, :].astype(jnp.float32))
            norm = found if norm is None else jnp.maximum(norm, found)
    return norm


def first_kernel(
    along, here_ref, order_ref, limit_ref, query_ref, dec_ref, pairs_ref, dec_query_ref, limits_ref, norms_ref, sums_ref, tops_ref, dec_rows
):
    rows, heads = query_ref.shape[0], query_ref.shape[1] // HD
    steps, share = dec_ref.shape[0], limits_ref.shape[0] // dec_ref.shape[0]
    first = here_ref[0] * share
    base = pl.multiple_of(first // TILE * TILE, TILE)
    for head in range(heads):
        for step in range(steps):
            block = dec_ref[step, pl.ds(base, TILE), head * HD : (head + 1) * HD].astype(jnp.float32)
            mine = block[0:share]
            for other in range(share, TILE, share):
                mine = jnp.where(first - base == other, block[other : other + share], mine)
            dec_rows[(head * steps + step) * share : (head * steps + step + 1) * share, :] = mine
    for step in range(steps):
        for row in range(share):
            limits_ref[step * share + row : step * share + row + 1, :] = jnp.full(
                (1, HD), limit_ref[step, first + row], jnp.int32
            )
    dec_query_ref[...] = dec_rows[...].astype(jnp.bfloat16)
    query_norm = largest_norm(dec_rows[...])
    for head in range(heads):
        query = query_ref[:, head * HD : (head + 1) * HD].astype(jnp.float32)
        query_norm = jnp.maximum(query_norm, largest_norm(query))
    query_norm = query_norm * (SCALE * SCALE)
    key_norm = key_norms((pairs_ref,), rows)
    norms_ref[0] = jnp.broadcast_to(query_norm, norms_ref.shape[1:])
    norms_ref[1] = jnp.broadcast_to(key_norm, norms_ref.shape[1:])
    calm = reach_of(query_norm, key_norm) <= REACH * REACH

    def emit(group, sums, top):
        sums_ref[group] = sums
        if top is not None:
            tops_ref[group] = top

    refs = (here_ref, order_ref, query_ref, dec_query_ref, limits_ref)
    attend(refs, (pairs_ref,), ((0, False),), along, calm, True, None, None, emit)


def norms_so_far(norms_ref, pairs_refs, rows):
    query_norm, before = norms_ref[0], norms_ref[1]
    now = jnp.maximum(before, key_norms(pairs_refs, rows))
    bound = REACH * REACH
    return now, reach_of(query_norm, now) <= bound, reach_of(query_norm, before) <= bound


def next_kernel(along, places_of, blocks, here_ref, order_ref, query_ref, dec_query_ref, limits_ref, norms_in, sums_in, tops_in, *rest):
    pairs_refs = rest[:blocks]
    norms_ref, sums_ref, tops_ref = rest[blocks:]
    now, calm, was_calm = norms_so_far(norms_in, pairs_refs, query_ref.shape[0])
    norms_ref[0] = norms_in[0]
    norms_ref[1] = now

    def emit(group, sums, top):
        sums_ref[group] = sums
        if top is not None:
            tops_ref[group] = top

    refs = (here_ref, order_ref, query_ref, dec_query_ref, limits_ref)
    attend(refs, pairs_refs, places_of, along, calm, was_calm, sums_in, tops_in, emit)


def last_kernel(along, places_of, taken, arrivals, here_ref, order_ref, owner_ref, query_ref, dec_query_ref, limits_ref, norms_in, sums_in, tops_in, *rest):
    pairs_refs, rest = rest[:taken], rest[taken:]
    places = len(arrivals)
    sources = rest[:places]
    (out_ref, owned_keys_ref, owned_values_ref, dec_out_ref, out_rows, dec_rows, out_sems, owned_sems, dec_sem) = rest[places:]
    rows, heads = query_ref.shape[0], query_ref.shape[1] // HD
    steps, share = dec_out_ref.shape[0], dec_out_ref.shape[1]
    here = here_ref[0]

    ranks = owner_ref.shape[0]
    slots = ranks // OWNERS
    owner, turn = here // slots, here % slots
    source, seen = jnp.int32(0), jnp.int32(0)
    for rank in range(ranks):
        match = owner_ref[rank] == owner
        source = jnp.where(jnp.logical_and(match, seen == turn), rank, source)
        seen = seen + match.astype(jnp.int32)
    offset = pl.multiple_of(jnp.where(source // along == here // along, 0, 2 * rows), 2 * rows)
    apart = lax.rem(source - here + 2 * along, along)

    def hand_over(block, start):
        return (
            pltpu.make_async_copy(block.at[pl.ds(start, rows), :], owned_keys_ref, owned_sems.at[0]),
            pltpu.make_async_copy(block.at[pl.ds(start + rows, rows), :], owned_values_ref, owned_sems.at[1]),
        )

    for block, distance in zip(sources, arrivals):

        @pl.when(apart == distance % along)
        def _(block=block):
            for copy in hand_over(block, offset):
                copy.start()

    def emit_head(group, mixed):
        out_rows[group] = mixed
        out_copy(group).start()

    def emit_decode(mixed):
        for head in range(heads):
            piece = mixed[head * steps * share : (head + 1) * steps * share]
            dec_rows[:, :, head * HD : (head + 1) * HD] = piece.reshape(steps, share, HD)
        dec_copy.start()

    def out_copy(group):
        across = pl.ds(pl.multiple_of(group * HD, HD), HD)
        return pltpu.make_async_copy(out_rows.at[group], out_ref.at[:, across], out_sems.at[group])

    dec_copy = pltpu.make_async_copy(dec_rows, dec_out_ref, dec_sem)

    def emit(group, sums, top):
        mixed = (sums[:, 0:HD] / sums[:, HD:]).astype(jnp.bfloat16)
        if top is None:
            emit_head(group, mixed) if group < heads else emit_decode(mixed)
        else:
            pl.when(group < heads)(lambda: emit_head(group, mixed))
            pl.when(group == heads)(lambda: emit_decode(mixed))

    def settle():
        for group in range(heads):
            out_copy(group).wait()
        dec_copy.wait()

    _, calm, was_calm = norms_so_far(norms_in, pairs_refs, rows)
    refs = (here_ref, order_ref, query_ref, dec_query_ref, limits_ref)
    attend(refs, pairs_refs, places_of, along, calm, was_calm, sums_in, tops_in, emit, settle)
    settle()
    for copy in hand_over(sources[0], 0):
        copy.wait()


def pack_kernel(keys_ref, values_ref, pair_ref, sems):
    rows = keys_ref.shape[0]
    copies = (
        pltpu.make_async_copy(keys_ref, pair_ref.at[0:rows], sems.at[0]),
        pltpu.make_async_copy(values_ref, pair_ref.at[rows : 2 * rows], sems.at[1]),
    )
    for copy in copies:
        copy.start()
    for copy in copies:
        copy.wait()


def per_device(queries, keys, values, block_order, owner_of, dec_queries, dec_pos):
    rows = queries.shape[0]
    heads = queries.shape[1] // HD
    groups = heads + 1
    ranks = lax.axis_size("ctx")
    here = lax.axis_index("ctx").astype(jnp.int32).reshape(1)
    along = ranks // HALVES
    share = DROWS // ranks

    def shift(block, by):
        moves = []
        for rank in range(ranks):
            half, place = rank // along, rank % along
            moves.append((rank, half * along + (place + by) % along))
        return lax.ppermute(block, "ctx", moves)

    swap = [(rank, (rank + along) % ranks) for rank in range(ranks)]
    own = pl.pallas_call(
        pack_kernel,
        in_specs=[pl.BlockSpec(memory_space=pl.ANY)] * 2,
        out_specs=pl.BlockSpec(memory_space=pltpu.VMEM),
        out_shape=pltpu.VMEM((2 * rows, HD), keys.dtype),
        scratch_shapes=[pltpu.SemaphoreType.DMA((2,))],
        name="pack",
    )(keys, values)
    other = lax.ppermute(own, "ctx", swap)
    local = jnp.concatenate([own, other], axis=0)
    rights, lefts = [local], [local]
    for step in range(1, along // 2):
        rights.append(shift(rights[-1], -1))
        lefts.append(shift(lefts[-1], 1))
    rounds = [{step: rights[step], -step: lefts[step]} for step in range(1, along // 2)]
    last = {along // 2: shift(rights[-1], -1)}

    smem = pl.BlockSpec(memory_space=pltpu.SMEM)
    vmem = pl.BlockSpec(memory_space=pltpu.VMEM)
    anywhere = pl.BlockSpec(memory_space=pl.ANY)
    shape = jax.ShapeDtypeStruct
    carried = [
        shape((2, 8, HD), jnp.float32),
        shape((groups, rows, 2 * HD), jnp.float32),
        shape((groups, rows, HD), jnp.float32),
    ]

    def cost(items):
        return pl.CostEstimate(
            flops=4 * 8 * groups * rows * items * rows * HD,
            bytes_accessed=items * rows * HD * 4,
            transcendentals=groups * rows * items * rows,
        )

    params = pltpu.CompilerParams(vmem_limit_bytes=24 * 2**20)
    dec_query, limits, *state = pl.pallas_call(
        functools.partial(first_kernel, along),
        in_specs=[smem] * 3 + [vmem] * 3,
        out_specs=[vmem] * 5,
        out_shape=[shape((rows, HD), jnp.bfloat16), shape((STEPS * share, HD), jnp.int32)] + carried,
        scratch_shapes=[pltpu.VMEM((rows, HD), jnp.float32)],
        compiler_params=params,
        cost_estimate=cost(1),
        name="attend_own",
    )(here, block_order, dec_pos, queries, dec_queries, own)
    fixed = (queries, dec_query, limits)

    def attend_more(state, blocks, places_of, name):
        return pl.pallas_call(
            functools.partial(next_kernel, along, places_of, len(blocks)),
            in_specs=[smem] * 2 + [vmem] * (6 + len(blocks)),
            out_specs=[vmem] * 3,
            out_shape=carried,
            compiler_params=params,
            cost_estimate=cost(max(len(places_of), 2 * HALVES)),
            name=name,
        )(here, block_order, *fixed, *state, *blocks)

    state = attend_more(state, [other], ((0, True),), "attend_other")
    def halves_of(blocks):
        return tuple((distance, other) for distance in blocks for other in (False, True))

    for number, blocks in enumerate(rounds):
        state = attend_more(state, list(blocks.values()), halves_of(blocks), f"attend_{number}")
    sources = {0: local}
    for blocks in rounds + [last]:
        sources.update(blocks)
    return pl.pallas_call(
        functools.partial(last_kernel, along, halves_of(last), len(last), tuple(sources)),
        in_specs=[smem] * 3 + [vmem] * (6 + len(last)) + [anywhere] * len(sources),
        out_specs=[anywhere] * 4,
        out_shape=[
            shape(queries.shape, queries.dtype),
            shape(keys.shape, keys.dtype),
            shape(values.shape, values.dtype),
            shape((STEPS, share, heads * HD), queries.dtype),
        ],
        scratch_shapes=[
            pltpu.VMEM((heads, rows, HD), jnp.bfloat16),
            pltpu.VMEM((STEPS, share, heads * HD), jnp.bfloat16),
            pltpu.SemaphoreType.DMA((heads,)),
            pltpu.SemaphoreType.DMA((2,)),
            pltpu.SemaphoreType.DMA(()),
        ],
        compiler_params=params,
        cost_estimate=cost(HALVES),
        name="attend_last",
    )(here, block_order, owner_of, *fixed, *state, *last.values(), *sources.values())


def solution(mesh):
    placed = (
        P(("req", "ctx"), "head"),
        P(("req", "ctx"), "head"),
        P(("req", "ctx"), "head"),
        P("req"),
        P("req"),
        P("req", None, "head"),
        P("req", None),
    )
    return jax.shard_map(
        per_device,
        mesh=mesh,
        in_specs=placed,
        out_specs=(
            P(("req", "ctx"), "head"),
            P(("req", "ctx"), "head"),
            P(("req", "ctx"), "head"),
            P("req", "ctx", "head"),
        ),
        check_vma=False,
    )
```

```python
import functools

import jax
import jax.numpy as jnp
from jax import lax
from jax.experimental import pallas as pl
from jax.experimental.pallas import tpu as pltpu
from jax.sharding import PartitionSpec as P

HD = 128
BLK = 128
DROWS = 128
STEPS = 4
OWNERS = 4
HALVES = 2
TILE = 16
TOGETHER = 2

LOWEST = -1e30
LOG2E = 1.4426950408889634
SCALE = LOG2E * HD ** (-0.5)
REACH = 64.0


def largest_norm(rows):
    lengths = jnp.sum(rows * rows, axis=1, keepdims=True)
    return jnp.max(lengths, axis=0, keepdims=True)


def attend(refs, pairs_refs, places_of, along, calm, was_calm, sums_ref, tops_ref, emit, settle=lambda: None):
    here_ref, order_ref, query_ref, dec_query_ref, limits_ref = refs
    rows, heads = query_ref.shape[0], query_ref.shape[1] // HD
    groups = heads + 1
    here = here_ref[0]
    lane = lax.broadcasted_iota(jnp.int32, (1, rows), 1)
    line = lax.broadcasted_iota(jnp.int32, (rows, HD), 0)

    def places(rank, index):
        low = order_ref[rank * 2] * BLK
        high = order_ref[rank * 2 + 1] * BLK - BLK
        return jnp.where(index < BLK, low, high) + index

    query_places = places(here, line)
    dec_places = jnp.tile(limits_ref[...] - 1, (heads, 1))
    blocks = [(ref, start) for ref in pairs_refs for start in range(0, ref.shape[0], 2 * rows)]
    items = []
    for (ref, start), (distance, other) in zip(blocks, places_of):
        half = here // along
        half = 1 - half if other else half
        rank = half * along + lax.rem(here + distance + along, along)
        items.append((ref, start, places(rank, lane)))

    def item_rows(part):
        keys = [ref[start : start + rows, :] for ref, start, _ in part]
        values = [ref[start + rows : start + 2 * rows, :] for ref, start, _ in part]
        wide = [jnp.concatenate([value, jnp.ones_like(value)], axis=1) for value in values]
        return jnp.concatenate(keys, axis=0), jnp.concatenate(wide, axis=0)

    def masked(query, keys, part, row_places):
        scores = lax.dot_general(query, keys, (((1,), (1,)), ((), ())), preferred_element_type=jnp.float32)
        key_places = jnp.concatenate([key_places for _, _, key_places in part], axis=1)
        visible = jnp.tile(row_places, (1, key_places.shape[1] // HD)) >= key_places
        return jnp.where(visible, scores * SCALE, LOWEST)

    parts = [items[first : first + TOGETHER] for first in range(0, len(items), TOGETHER)]

    def start_sums(group):
        return jnp.zeros((rows, 2 * HD), jnp.float32) if sums_ref is None else sums_ref[group]

    for group in [heads, *range(heads)]:
        row_places = query_places if group < heads else dec_places
        query = query_ref[:, group * HD : (group + 1) * HD] if group < heads else dec_query_ref[...]
        sums = start_sums(group)
        for part in parts:
            keys, wide = item_rows(part)
            weights = jnp.exp2(masked(query, keys, part, row_places))
            sums += jnp.dot(weights.astype(jnp.bfloat16), wide, preferred_element_type=jnp.float32)
        emit(group, sums, None)

    @pl.when(jnp.logical_not(calm))
    def _():
        settle()

        def visit(group, _):
            row_places = jnp.where(group < heads, query_places, dec_places)
            across = pl.ds(pl.multiple_of(jnp.minimum(group, heads - 1) * HD, HD), HD)
            query = jnp.where(group < heads, query_ref[:, across], dec_query_ref[...])
            sums = start_sums(group)
            top = jnp.where(sums[:, HD:] > 0.0, 0.0, LOWEST)
            if tops_ref is not None:
                top = jnp.where(was_calm, top, tops_ref[group])
            for part in parts:
                keys, wide = item_rows(part)
                scores = masked(query, keys, part, row_places)
                new_top = jnp.maximum(top, jnp.max(scores, axis=1, keepdims=True))
                weights = jnp.exp2(scores - jnp.tile(new_top, (1, scores.shape[1] // HD)))
                fade = jnp.tile(jnp.exp2(top - new_top), (1, 2))
                sums = sums * fade + jnp.dot(
                    weights.astype(jnp.bfloat16), wide, preferred_element_type=jnp.float32
                )
                top = new_top
            emit(group, sums, top)
            return 0

        lax.fori_loop(0, groups, visit, 0)


def reach_of(query_norm, key_norm):
    return jnp.max(query_norm * key_norm)


def key_norms(pairs_refs, rows):
    norm = None
    for ref in pairs_refs:
        for start in range(0, ref.shape[0], 2 * rows):
            found = largest_norm(ref[start : start + rows, :].astype(jnp.float32))
            norm = found if norm is None else jnp.maximum(norm, found)
    return norm


def first_kernel(
    along, here_ref, order_ref, limit_ref, query_ref, dec_ref, pairs_ref, dec_query_ref, limits_ref, norms_ref, sums_ref, tops_ref, dec_rows
):
    rows, heads = query_ref.shape[0], query_ref.shape[1] // HD
    steps, share = dec_ref.shape[0], limits_ref.shape[0] // dec_ref.shape[0]
    first = here_ref[0] * share
    base = pl.multiple_of(first // TILE * TILE, TILE)
    for head in range(heads):
        for step in range(steps):
            block = dec_ref[step, pl.ds(base, TILE), head * HD : (head + 1) * HD].astype(jnp.float32)
            mine = block[0:share]
            for other in range(share, TILE, share):
                mine = jnp.where(first - base == other, block[other : other + share], mine)
            dec_rows[(head * steps + step) * share : (head * steps + step + 1) * share, :] = mine
    for step in range(steps):
        for row in range(share):
            limits_ref[step * share + row : step * share + row + 1, :] = jnp.full(
                (1, HD), limit_ref[step, first + row], jnp.int32
            )
    dec_query_ref[...] = dec_rows[...].astype(jnp.bfloat16)
    query_norm = largest_norm(dec_rows[...])
    for head in range(heads):
        query = query_ref[:, head * HD : (head + 1) * HD].astype(jnp.float32)
        query_norm = jnp.maximum(query_norm, largest_norm(query))
    query_norm = query_norm * (SCALE * SCALE)
    key_norm = key_norms((pairs_ref,), rows)
    norms_ref[0] = jnp.broadcast_to(query_norm, norms_ref.shape[1:])
    norms_ref[1] = jnp.broadcast_to(key_norm, norms_ref.shape[1:])
    calm = reach_of(query_norm, key_norm) <= REACH * REACH

    def emit(group, sums, top):
        sums_ref[group] = sums
        if top is not None:
            tops_ref[group] = top

    refs = (here_ref, order_ref, query_ref, dec_query_ref, limits_ref)
    attend(refs, (pairs_ref,), ((0, False),), along, calm, True, None, None, emit)


def norms_so_far(norms_ref, pairs_refs, rows):
    query_norm, before = norms_ref[0], norms_ref[1]
    now = jnp.maximum(before, key_norms(pairs_refs, rows))
    bound = REACH * REACH
    return now, reach_of(query_norm, now) <= bound, reach_of(query_norm, before) <= bound


def next_kernel(along, places_of, blocks, here_ref, order_ref, query_ref, dec_query_ref, limits_ref, norms_in, sums_in, tops_in, *rest):
    pairs_refs = rest[:blocks]
    norms_ref, sums_ref, tops_ref = rest[blocks:]
    now, calm, was_calm = norms_so_far(norms_in, pairs_refs, query_ref.shape[0])
    norms_ref[0] = norms_in[0]
    norms_ref[1] = now

    def emit(group, sums, top):
        sums_ref[group] = sums
        if top is not None:
            tops_ref[group] = top

    refs = (here_ref, order_ref, query_ref, dec_query_ref, limits_ref)
    attend(refs, pairs_refs, places_of, along, calm, was_calm, sums_in, tops_in, emit)


def last_kernel(along, places_of, taken, arrivals, here_ref, order_ref, owner_ref, query_ref, dec_query_ref, limits_ref, norms_in, sums_in, tops_in, *rest):
    pairs_refs, rest = rest[:taken], rest[taken:]
    places = len(arrivals)
    sources = rest[:places]
    (out_ref, owned_keys_ref, owned_values_ref, dec_out_ref, out_rows, dec_rows, out_sems, owned_sems, dec_sem) = rest[places:]
    rows, heads = query_ref.shape[0], query_ref.shape[1] // HD
    steps, share = dec_out_ref.shape[0], dec_out_ref.shape[1]
    here = here_ref[0]

    ranks = owner_ref.shape[0]
    slots = ranks // OWNERS
    owner, turn = here // slots, here % slots
    source, seen = jnp.int32(0), jnp.int32(0)
    for rank in range(ranks):
        match = owner_ref[rank] == owner
        source = jnp.where(jnp.logical_and(match, seen == turn), rank, source)
        seen = seen + match.astype(jnp.int32)
    offset = pl.multiple_of(jnp.where(source // along == here // along, 0, 2 * rows), 2 * rows)
    apart = lax.rem(source - here + 2 * along, along)

    def hand_over(block, start):
        return (
            pltpu.make_async_copy(block.at[pl.ds(start, rows), :], owned_keys_ref, owned_sems.at[0]),
            pltpu.make_async_copy(block.at[pl.ds(start + rows, rows), :], owned_values_ref, owned_sems.at[1]),
        )

    for block, distance in zip(sources, arrivals):

        @pl.when(apart == distance % along)
        def _(block=block):
            for copy in hand_over(block, offset):
                copy.start()

    def emit_head(group, mixed):
        out_rows[group] = mixed
        out_copy(group).start()

    def emit_decode(mixed):
        for head in range(heads):
            piece = mixed[head * steps * share : (head + 1) * steps * share]
            dec_rows[:, :, head * HD : (head + 1) * HD] = piece.reshape(steps, share, HD)
        dec_copy.start()

    def out_copy(group):
        across = pl.ds(pl.multiple_of(group * HD, HD), HD)
        return pltpu.make_async_copy(out_rows.at[group], out_ref.at[:, across], out_sems.at[group])

    dec_copy = pltpu.make_async_copy(dec_rows, dec_out_ref, dec_sem)

    def emit(group, sums, top):
        mixed = (sums[:, 0:HD] / sums[:, HD:]).astype(jnp.bfloat16)
        if top is None:
            emit_head(group, mixed) if group < heads else emit_decode(mixed)
        else:
            pl.when(group < heads)(lambda: emit_head(group, mixed))
            pl.when(group == heads)(lambda: emit_decode(mixed))

    def settle():
        for group in range(heads):
            out_copy(group).wait()
        dec_copy.wait()

    _, calm, was_calm = norms_so_far(norms_in, pairs_refs, rows)
    refs = (here_ref, order_ref, query_ref, dec_query_ref, limits_ref)
    attend(refs, pairs_refs, places_of, along, calm, was_calm, sums_in, tops_in, emit, settle)
    settle()
    for copy in hand_over(sources[0], 0):
        copy.wait()


def pack_kernel(keys_ref, values_ref, pair_ref, sems):
    rows = keys_ref.shape[0]
    copies = (
        pltpu.make_async_copy(keys_ref, pair_ref.at[0:rows], sems.at[0]),
        pltpu.make_async_copy(values_ref, pair_ref.at[rows : 2 * rows], sems.at[1]),
    )
    for copy in copies:
        copy.start()
    for copy in copies:
        copy.wait()


def per_device(queries, keys, values, block_order, owner_of, dec_queries, dec_pos):
    rows = queries.shape[0]
    heads = queries.shape[1] // HD
    groups = heads + 1
    ranks = lax.axis_size("ctx")
    here = lax.axis_index("ctx").astype(jnp.int32).reshape(1)
    along = ranks // HALVES
    share = DROWS // ranks

    def shift(block, by):
        moves = []
        for rank in range(ranks):
            half, place = rank // along, rank % along
            moves.append((rank, half * along + (place + by) % along))
        return lax.ppermute(block, "ctx", moves)

    swap = [(rank, (rank + along) % ranks) for rank in range(ranks)]
    own = pl.pallas_call(
        pack_kernel,
        in_specs=[pl.BlockSpec(memory_space=pl.ANY)] * 2,
        out_specs=pl.BlockSpec(memory_space=pltpu.VMEM),
        out_shape=pltpu.VMEM((2 * rows, HD), keys.dtype),
        scratch_shapes=[pltpu.SemaphoreType.DMA((2,))],
        name="pack",
    )(keys, values)
    other = lax.ppermute(own, "ctx", swap)
    local = jnp.concatenate([own, other], axis=0)
    rights, lefts = [local], [local]
    for step in range(1, along // 2):
        rights.append(shift(rights[-1], -1))
        lefts.append(shift(lefts[-1], 1))
    rounds = [{step: rights[step], -step: lefts[step]} for step in range(1, along // 2)]
    last = {along // 2: shift(rights[-1], -1)}

    smem = pl.BlockSpec(memory_space=pltpu.SMEM)
    vmem = pl.BlockSpec(memory_space=pltpu.VMEM)
    anywhere = pl.BlockSpec(memory_space=pl.ANY)
    shape = jax.ShapeDtypeStruct
    carried = [
        shape((2, 8, HD), jnp.float32),
        shape((groups, rows, 2 * HD), jnp.float32),
        shape((groups, rows, HD), jnp.float32),
    ]

    def cost(items):
        return pl.CostEstimate(
            flops=4 * 8 * groups * rows * items * rows * HD,
            bytes_accessed=items * rows * HD * 4,
            transcendentals=groups * rows * items * rows,
        )

    params = pltpu.CompilerParams(vmem_limit_bytes=24 * 2**20)
    dec_query, limits, *state = pl.pallas_call(
        functools.partial(first_kernel, along),
        in_specs=[smem] * 3 + [vmem] * 3,
        out_specs=[vmem] * 5,
        out_shape=[shape((rows, HD), jnp.bfloat16), shape((STEPS * share, HD), jnp.int32)] + carried,
        scratch_shapes=[pltpu.VMEM((rows, HD), jnp.float32)],
        compiler_params=params,
        cost_estimate=cost(1),
        name="attend_own",
    )(here, block_order, dec_pos, queries, dec_queries, own)
    fixed = (queries, dec_query, limits)

    def attend_more(state, blocks, places_of, name):
        return pl.pallas_call(
            functools.partial(next_kernel, along, places_of, len(blocks)),
            in_specs=[smem] * 2 + [vmem] * (6 + len(blocks)),
            out_specs=[vmem] * 3,
            out_shape=carried,
            compiler_params=params,
            cost_estimate=cost(max(len(places_of), 2 * HALVES)),
            name=name,
        )(here, block_order, *fixed, *state, *blocks)

    state = attend_more(state, [other], ((0, True),), "attend_other")
    def halves_of(blocks):
        return tuple((distance, other) for distance in blocks for other in (False, True))

    for number, blocks in enumerate(rounds):
        state = attend_more(state, list(blocks.values()), halves_of(blocks), f"attend_{number}")
    sources = {0: local}
    for blocks in rounds + [last]:
        sources.update(blocks)
    return pl.pallas_call(
        functools.partial(last_kernel, along, halves_of(last), len(last), tuple(sources)),
        in_specs=[smem] * 3 + [vmem] * (6 + len(last)) + [anywhere] * len(sources),
        out_specs=[anywhere] * 4,
        out_shape=[
            shape(queries.shape, queries.dtype),
            shape(keys.shape, keys.dtype),
            shape(values.shape, values.dtype),
            shape((STEPS, share, heads * HD), queries.dtype),
        ],
        scratch_shapes=[
            pltpu.VMEM((heads, rows, HD), jnp.bfloat16),
            pltpu.VMEM((STEPS, share, heads * HD), jnp.bfloat16),
            pltpu.SemaphoreType.DMA((heads,)),
            pltpu.SemaphoreType.DMA((2,)),
            pltpu.SemaphoreType.DMA(()),
        ],
        compiler_params=params,
        cost_estimate=cost(HALVES),
        name="attend_last",
    )(here, block_order, owner_of, *fixed, *state, *last.values(), *sources.values())


def solution(mesh):
    placed = (
        P(("req", "ctx"), "head"),
        P(("req", "ctx"), "head"),
        P(("req", "ctx"), "head"),
        P("req"),
        P("req"),
        P("req", None, "head"),
        P("req", None),
    )
    return jax.shard_map(
        per_device,
        mesh=mesh,
        in_specs=placed,
        out_specs=(
            P(("req", "ctx"), "head"),
            P(("req", "ctx"), "head"),
            P(("req", "ctx"), "head"),
            P("req", "ctx", "head"),
        ),
        check_vma=False,
    )
```
